32 devices in a mesh: group: 8 (over y, x, core), blk: 4 (over z).
Axes of the slice: x: 2, y: 2, z: 4, core: 2. Of those that a mesh axis runs over, the one named last changes fastest.
Arguments:
- embedding: bfloat16 [4096, 1024], P(('group', 'blk'))
- cluster: int32 [4096], P(('group', 'blk')), may hold values from 0 to 127, as said below
- doc_index: int32 [4096], P(('group', 'blk')), may hold values from 0 to 4095, each once
Outputs:
- best_cosine: float32 [4096], P(('group', 'blk'))
The draws below stay inside these ranges and needn't reach their ends.
Inputs may be any that keep to these rules, and one draw needn't show every extreme that they name: `cluster`: cluster c is owned by group c mod 8. The 128 documents of one device send at most 32 documents to one owner group; a quarter of the groups receive exactly 32 from every device.
All inputs are finite; a program needn't handle non-finite values.
Results may differ from the reference program's by a relative error of at most 0.00067.
Values may be sent and summed in bfloat16 or wider, within the bound.
No kernel may reach another device: no remote copies, remote signals or barrier semaphores. Data moves between devices by JAX's collectives and lax.ppermute only.
A program may use at most 64 MiB of HBM per device.

```python
import math
import jax
import jax.numpy as jnp
from jax import lax

D = 1024
ROWS = 128
CPG = 16
N = 4096
CLUSTERS = 128
GROUP_CAP = 1024
N_GROUP = 8


def draw_embedding(key, part):
    key_base, key_scale = jax.random.split(key, 2)
    base = jax.random.normal(key_base, (N, D), jnp.float32)
    scale = jnp.exp(jax.random.uniform(key_scale, (N, 1), jnp.float32, 0.0, math.log(10.0)))
    return (base * scale).astype(jnp.bfloat16)


def draw_cluster(key, part):
    groups = CLUSTERS // CPG
    devices = N // ROWS
    mean_rows = ROWS // groups
    key_hot, key_rest, key_rows, key_one, key_two = jax.random.split(key, 5)
    hot_rank = jax.random.permutation(key_hot, groups)
    is_hot = hot_rank < groups // 4
    positions = jnp.arange(groups, dtype=jnp.int32)
    levels = jnp.where(positions < groups // 4, 2 * mean_rows, jnp.where(positions < 3 * groups // 4, mean_rows, 0)).astype(jnp.int32)

    def one_device(rest_key, row_key):
        ranks = jax.random.permutation(rest_key, groups).astype(jnp.int32)
        sort_key = jnp.where(is_hot, -1, ranks).astype(jnp.int32)
        order = jnp.argsort(sort_key, stable=True).astype(jnp.int32)
        counts = jnp.zeros((groups,), jnp.int32).at[order].set(levels)
        bounds = jnp.cumsum(counts)
        row_group = jnp.searchsorted(bounds, jnp.arange(ROWS, dtype=jnp.int32), side='right').astype(jnp.int32)
        return row_group[jax.random.permutation(row_key, ROWS)]
    dest = jax.vmap(one_device)(jax.random.split(key_rest, devices), jax.random.split(key_rows, devices)).reshape(N)
    first = jax.random.randint(key_one, (N,), 0, CPG)
    second = jax.random.randint(key_two, (N,), 0, CPG)
    within = jnp.minimum(first, second)
    return (dest + groups * within).astype(jnp.int32)


def setup_inputs(seed: int = 0) -> dict:
    splits = jax.random.split(jax.random.key(seed), 4)
    return {
        "embedding": draw_embedding(jax.random.fold_in(splits[3], 71), 0),
        "cluster": draw_cluster(jax.random.fold_in(splits[3], 71), 0),
        "doc_index": jax.random.permutation(splits[2], N).astype(jnp.int32),
    }


def reference(embedding, cluster, doc_index):
    wide = embedding.astype(jnp.float32)
    unit = (wide * lax.rsqrt(lax.optimization_barrier(jnp.sum(wide * wide, axis=1, keepdims=True)) + 1e-06)).astype(jnp.bfloat16)
    owner = cluster % N_GROUP
    block = 512 if GROUP_CAP % 512 == 0 else GROUP_CAP
    nblocks = GROUP_CAP // block

    def one_group(group_id):
        flags = jnp.where(owner == group_id, 0, 1).astype(jnp.int32)
        order = jnp.argsort(flags, stable=True)[:GROUP_CAP].astype(jnp.int32)
        rows_unit = unit[order]
        rows_clu = cluster[order]
        rows_idx = doc_index[order]
        valid = owner[order] == group_id

        def one_block(number):
            start = (number * block).astype(jnp.int32)
            query = lax.dynamic_slice_in_dim(rows_unit, start, block, 0)
            q_clu = lax.dynamic_slice_in_dim(rows_clu, start, block, 0)
            q_idx = lax.dynamic_slice_in_dim(rows_idx, start, block, 0)
            scores = jnp.dot(query, rows_unit.T, preferred_element_type=jnp.float32)
            allowed = (rows_clu[None, :] == q_clu[:, None]) & (rows_idx[None, :] < q_idx[:, None])
            return lax.optimization_barrier(jnp.max(jnp.where(allowed, scores, jnp.float32(-1.0)), axis=1))
        best = lax.map(one_block, jnp.arange(nblocks, dtype=jnp.int32)).reshape(GROUP_CAP)
        return (order, jnp.where(valid, best, jnp.float32(-1.0)))
    orders, bests = lax.map(one_group, jnp.arange(N_GROUP, dtype=jnp.int32))
    result = jnp.full((N,), -1.0, jnp.float32)
    return result.at[orders.reshape(-1)].max(bests.reshape(-1))
```

```python
import functools

import jax
import jax.numpy as jnp
from jax import lax
from jax.experimental import pallas as pl
from jax.experimental.pallas import tpu as pltpu
from jax.sharding import PartitionSpec as P

LANES = 128
META = 16


def pack_kernel(emb_a, clu_a, idx_a, emb_b, clu_b, idx_b, out):
    width = emb_a.shape[1]
    for half, (emb, clu, idx) in enumerate(((emb_a, clu_a, idx_a), (emb_b, clu_b, idx_b))):
        base = half * (width + META)
        wide = emb[...].astype(jnp.float32)
        norm = lax.rsqrt(jnp.sum(wide * wide, axis=1, keepdims=True) + 1e-06)
        unit = (wide * norm).astype(jnp.bfloat16)
        for k in range(width // LANES):
            out[pl.ds(base + k * LANES, LANES), :] = unit[:, k * LANES : (k + 1) * LANES]
        row = lax.broadcasted_iota(jnp.int32, (META, LANES), 0)
        index = idx[...]
        meta = jnp.where(row == 0, clu[...], jnp.where(row == 1, index >> 8, index & 255))
        out[pl.ds(base + width, META), :] = meta.astype(jnp.float32).astype(jnp.bfloat16)


def load_block(ref, base, width):
    parts = [ref[pl.ds(base + k * LANES, LANES), :] for k in range(width // LANES)]
    meta = ref[pl.ds(base + width, META), :].astype(jnp.float32)
    return jnp.concatenate(parts, axis=1), meta[0:1], meta[1:2] * 256.0 + meta[2:3]


def down(row):
    return jnp.transpose(jnp.broadcast_to(row, (LANES, LANES)))


def score_kernel(places, queries, cross, *refs):
    nkeys = 1 + max(place[0] for place in places)
    query_ref, key_refs, outs = refs[0], refs[1 : 1 + nkeys], refs[1 + nkeys :]
    step = query_ref.shape[0] // 2
    width = step - META
    loaded = [load_block(query_ref, i * step, width) for i in range(queries)]
    query = jnp.concatenate([block[0] for block in loaded], axis=0)
    q_clu = jnp.concatenate([down(block[1]) for block in loaded], axis=0)
    q_idx = jnp.concatenate([down(block[2]) for block in loaded], axis=0)
    row_best = jnp.full((queries * LANES, LANES), -1.0, jnp.float32)
    for first in range(0, len(places), 2):
        pair = places[first : first + 2]
        keys = [load_block(key_refs[place[0]], place[1] * step, width) for place in pair]
        scores = lax.dot_general(
            query,
            jnp.concatenate([key[0] for key in keys], axis=0),
            (((1,), (1,)), ((), ())),
            preferred_element_type=jnp.float32,
        )
        for number, (place, key) in enumerate(zip(pair, keys)):
            part = scores[:, number * LANES : (number + 1) * LANES]
            part = jnp.where(key[1] == q_clu, part, -1.0)
            earlier = key[2] < q_idx
            row_best = jnp.maximum(row_best, jnp.where(earlier, part, -1.0))
            if cross:
                col = jnp.max(jnp.where(earlier, -1.0, part), axis=0, keepdims=True)
                outs[1][pl.ds(place[2], 1), :] = col
    for i in range(queries):
        block = jnp.transpose(row_best[i * LANES : (i + 1) * LANES])
        outs[0][pl.ds(i, 1), :] = jnp.max(block, axis=0, keepdims=True)


def score(places, queries, query, keys, cross):
    blocks = len(places)
    width = query.shape[0] // 2 - META
    shapes = [jax.ShapeDtypeStruct((queries, LANES), jnp.float32)]
    if cross:
        shapes.append(jax.ShapeDtypeStruct((blocks, LANES), jnp.float32))
    return pl.pallas_call(
        functools.partial(score_kernel, places, queries, cross),
        out_shape=shapes,
        in_specs=[pl.BlockSpec(memory_space=pltpu.VMEM)] * (1 + len(keys)),
        out_specs=[pl.BlockSpec(memory_space=pltpu.VMEM)] * len(shapes),
        compiler_params=pltpu.CompilerParams(vmem_limit_bytes=32 * 2**20),
        cost_estimate=pl.CostEstimate(
            flops=2 * queries * blocks * LANES * LANES * width,
            bytes_accessed=2 * (queries + blocks) * LANES * width,
            transcendentals=0,
        ),
    )(query, *keys)


def program(groups, blks, embedding, cluster, doc_index):
    rows, width = embedding.shape

    def swap(x):
        return lax.ppermute(x, "group", [(g, g ^ 1) for g in range(groups)])

    def turn(x, even, odd):
        return lax.ppermute(x, "group", [(g, g ^ (odd if g & 1 else even)) for g in range(groups)])

    order = [i // 2 if i % 2 == 0 else blks - 1 - i // 2 for i in range(blks)]
    rounds = max(1, blks // 4)

    def visit(x, number, back):
        pairs = []
        for g in range(groups):
            shift = number + 1 + (rounds if g & 1 else 0)
            for i in range(blks):
                a, b = order[i], order[(i + shift) % blks]
                a, b = g * blks + a, g * blks + b
                pairs.append((b, a) if back else (a, b))
        return lax.ppermute(x, ("group", "blk"), pairs)

    clu, idx = cluster.reshape(1, rows), doc_index.reshape(1, rows)
    pair = pl.pallas_call(
        pack_kernel,
        out_shape=jax.ShapeDtypeStruct((2 * (width + META), LANES), jnp.bfloat16),
        in_specs=[pl.BlockSpec(memory_space=pltpu.VMEM)] * 6,
        out_specs=pl.BlockSpec(memory_space=pltpu.VMEM),
        compiler_params=pltpu.CompilerParams(vmem_limit_bytes=16 * 2**20),
    )(
        embedding,
        clu,
        idx,
        swap(embedding),
        swap(cluster).reshape(1, rows),
        swap(doc_index).reshape(1, rows),
    )
    step = width + META

    near = turn(pair, 2, 4)
    visitors = [visit(pair, number, False) for number in range(rounds)]
    far = turn(near[:step], 4, 2)
    near_other = swap(near)
    far_other = swap(far)
    keys = [pair, near, near_other, far, far_other]
    places = [(0, 0, 0), (0, 1, 1), (1, 0, 2), (1, 1, 3), (2, 1, 4), (2, 0, 5), (3, 0, 6), (4, 0, 7)]
    bit = 8
    while bit < groups:
        places = places + [(a + len(keys), b, p + bit) for a, b, p in places]
        keys = keys + [lax.ppermute(k, "group", [(g, g ^ bit) for g in range(groups)]) for k in keys]
        bit *= 2

    (own_best,) = score(places, 1, pair, keys, False)
    rows_back, cols = [], None
    for number, visitor in enumerate(visitors):
        row_best, col_best = score(places, 2, visitor, keys, True)
        rows_back.append(row_best)
        cols = col_best if cols is None else jnp.maximum(cols, col_best)

    bit = groups // 2
    while bit > 1:
        even, odd = bit, {2: 4, 4: 2}.get(bit, bit)
        cols = jnp.maximum(cols[:bit], turn(cols[bit:], even, odd))
        bit //= 2
    chip = cols
    for number, row_best in enumerate(rows_back):
        chip = jnp.maximum(chip, visit(row_best, number, True))
    other = swap(chip[1])
    return jnp.maximum(jnp.maximum(own_best[0], chip[0]), other)


def solution(mesh):
    return jax.shard_map(
        functools.partial(program, mesh.shape["group"], mesh.shape["blk"]),
        mesh=mesh,
        in_specs=(P(("group", "blk"), None), P(("group", "blk")), P(("group", "blk"))),
        out_specs=P(("group", "blk")),
        check_vma=False,
    )
```

```python
import functools

import jax
import jax.numpy as jnp
from jax import lax
from jax.experimental import pallas as pl
from jax.experimental.pallas import tpu as pltpu
from jax.sharding import PartitionSpec as P

LANES = 128
META = 16


def pack_kernel(emb, clu, idx, out):
    width = emb.shape[1]
    wide = emb[...].astype(jnp.float32)
    norm = lax.rsqrt(jnp.sum(wide * wide, axis=1, keepdims=True) + 1e-06)
    unit = (wide * norm).astype(jnp.bfloat16)
    for k in range(width // LANES):
        out[pl.ds(k * LANES, LANES), :] = unit[:, k * LANES : (k + 1) * LANES]
    row = lax.broadcasted_iota(jnp.int32, (META, LANES), 0)
    index = idx[...]
    meta = jnp.where(row == 0, clu[...], jnp.where(row == 1, index >> 8, index & 255))
    out[pl.ds(width, META), :] = meta.astype(jnp.float32).astype(jnp.bfloat16)


def load_block(ref):
    width = ref.shape[0] - META
    parts = [ref[pl.ds(k * LANES, LANES), :] for k in range(width // LANES)]
    meta = ref[pl.ds(width, META), :].astype(jnp.float32)
    return jnp.concatenate(parts, axis=1), meta[0:1], meta[1:2] * 256.0 + meta[2:3]


def down(row):
    return jnp.transpose(jnp.broadcast_to(row, (LANES, LANES)))


def pair_kernel(block, mate, pair):
    step = block.shape[0]
    pair[pl.ds(0, step), :] = block[...]
    pair[pl.ds(step, step), :] = mate[...]


def join(block, mate):
    return pl.pallas_call(
        pair_kernel,
        out_shape=jax.ShapeDtypeStruct((2 * block.shape[0], LANES), block.dtype),
        in_specs=[pl.BlockSpec(memory_space=pltpu.VMEM)] * 2,
        out_specs=pl.BlockSpec(memory_space=pltpu.VMEM),
        compiler_params=pltpu.CompilerParams(vmem_limit_bytes=16 * 2**20),
    )(block, mate)


def score_kernel(queries, places, cross, *refs):
    query_ref, refs = refs[0], refs[1:]
    key_refs, outs = refs[: len(places)], refs[len(places) :]
    step = query_ref.shape[0] // queries
    loaded = [load_block(query_ref.at[pl.ds(i * step, step)]) for i in range(queries)]
    query = jnp.concatenate([block[0] for block in loaded], axis=0)
    q_clu = jnp.concatenate([down(block[1]) for block in loaded], axis=0)
    q_idx = jnp.concatenate([down(block[2]) for block in loaded], axis=0)
    row_best = jnp.full((queries * LANES, LANES), -1.0, jnp.float32)
    for first in range(0, len(places), 2):
        keys = [load_block(ref) for ref in key_refs[first : first + 2]]
        scores = lax.dot_general(
            query,
            jnp.concatenate([key[0] for key in keys], axis=0),
            (((1,), (1,)), ((), ())),
            preferred_element_type=jnp.float32,
        )
        for number, key in enumerate(keys):
            part = scores[:, number * LANES : (number + 1) * LANES]
            part = jnp.where(key[1] == q_clu, part, -1.0)
            earlier = key[2] < q_idx
            row_best = jnp.maximum(row_best, jnp.where(earlier, part, -1.0))
            if cross:
                col = jnp.max(jnp.where(earlier, -1.0, part), axis=0, keepdims=True)
                outs[1][pl.ds(places[first + number], 1), :] = col
    for i in range(queries):
        block = jnp.transpose(row_best[i * LANES : (i + 1) * LANES])
        outs[0][pl.ds(i, 1), :] = jnp.max(block, axis=0, keepdims=True)


def score(count, query, keys, places, cross):
    blocks = len(keys)
    width = keys[0].shape[0] - META
    shapes = [jax.ShapeDtypeStruct((count, LANES), jnp.float32)]
    if cross:
        shapes.append(jax.ShapeDtypeStruct((blocks, LANES), jnp.float32))
    return pl.pallas_call(
        functools.partial(score_kernel, count, places, cross),
        out_shape=shapes,
        in_specs=[pl.BlockSpec(memory_space=pltpu.VMEM)] * (1 + blocks),
        out_specs=[pl.BlockSpec(memory_space=pltpu.VMEM)] * len(shapes),
        compiler_params=pltpu.CompilerParams(vmem_limit_bytes=32 * 2**20),
        cost_estimate=pl.CostEstimate(
            flops=2 * count * blocks * LANES * LANES * width,
            bytes_accessed=2 * (count + blocks) * LANES * width,
            transcendentals=0,
        ),
    )(query, *keys)


def program(groups, blks, embedding, cluster, doc_index):
    rows, width = embedding.shape

    def swap(x):
        return lax.ppermute(x, "group", [(g, g ^ 1) for g in range(groups)])

    def turn(x, even, odd):
        return lax.ppermute(x, "group", [(g, g ^ (odd if g & 1 else even)) for g in range(groups)])

    order = [i // 2 if i % 2 == 0 else blks - 1 - i // 2 for i in range(blks)]
    rounds = max(1, blks // 4)

    def visit(x, number, back):
        pairs = []
        for g in range(groups):
            shift = number + 1 + (rounds if g & 1 else 0)
            for i in range(blks):
                a, b = order[i], order[(i + shift) % blks]
                a, b = g * blks + a, g * blks + b
                pairs.append((b, a) if back else (a, b))
        return lax.ppermute(x, ("group", "blk"), pairs)

    block = pl.pallas_call(
        pack_kernel,
        out_shape=jax.ShapeDtypeStruct((width + META, LANES), jnp.bfloat16),
        in_specs=[pl.BlockSpec(memory_space=pltpu.VMEM)] * 3,
        out_specs=pl.BlockSpec(memory_space=pltpu.VMEM),
        compiler_params=pltpu.CompilerParams(vmem_limit_bytes=16 * 2**20),
    )(embedding, cluster.reshape(1, rows), doc_index.reshape(1, rows))

    mate = swap(block)
    near = turn(block, 2, 4)
    pair = join(block, mate)
    visitors = [visit(pair, number, False) for number in range(rounds)]
    near_mate = turn(mate, 2, 4)
    far = turn(near, 4, 2)
    keys = [block, mate, near, near_mate, swap(near_mate), swap(near), far, swap(far)]
    places = [0, 1, 2, 3, 4, 5, 6, 7]
    bit = 8
    while bit < groups:
        keys = keys + [lax.ppermute(k, "group", [(g, g ^ bit) for g in range(groups)]) for k in keys]
        places = places + [p + bit for p in places]
        bit *= 2

    (own_best,) = score(1, block, keys, places, False)
    rows_back, cols = [], None
    for number, visitor in enumerate(visitors):
        row_best, col_best = score(2, visitor, keys, places, True)
        rows_back.append(row_best)
        cols = col_best if cols is None else jnp.maximum(cols, col_best)

    bit = groups // 2
    while bit > 1:
        even, odd = bit, {2: 4, 4: 2}.get(bit, bit)
        cols = jnp.maximum(cols[:bit], turn(cols[bit:], even, odd))
        bit //= 2
    chip = cols
    for number, row_best in enumerate(rows_back):
        chip = jnp.maximum(chip, visit(row_best, number, True))
    other = swap(chip[1])
    return jnp.maximum(jnp.maximum(own_best[0], chip[0]), other)


def solution(mesh):
    return jax.shard_map(
        functools.partial(program, mesh.shape["group"], mesh.shape["blk"]),
        mesh=mesh,
        in_specs=(P(("group", "blk"), None), P(("group", "blk")), P(("group", "blk"))),
        out_specs=P(("group", "blk")),
        check_vma=False,
    )
```

```python
import functools

import jax
import jax.numpy as jnp
from jax import lax
from jax.experimental import pallas as pl
from jax.experimental.pallas import tpu as pltpu
from jax.sharding import PartitionSpec as P

LANES = 128
META = 16


def pack_kernel(emb_hbm, clu_hbm, idx_hbm, out, emb, clu, idx, sems):
    width = emb.shape[1]
    copies = [
        pltpu.make_async_copy(source, target, sems.at[i])
        for i, (source, target) in enumerate(((emb_hbm, emb), (clu_hbm, clu), (idx_hbm, idx)))
    ]
    for copy in copies:
        copy.start()
    for copy in copies:
        copy.wait()
    wide = emb[...].astype(jnp.float32)
    norm = lax.rsqrt(jnp.sum(wide * wide, axis=1, keepdims=True) + 1e-06)
    unit = (wide * norm).astype(jnp.bfloat16)
    for k in range(width // LANES):
        out[pl.ds(k * LANES, LANES), :] = unit[:, k * LANES : (k + 1) * LANES]
    row = lax.broadcasted_iota(jnp.int32, (META, LANES), 0)
    index = idx[...]
    meta = jnp.where(row == 0, clu[...], jnp.where(row == 1, index >> 8, index & 255))
    out[pl.ds(width, META), :] = meta.astype(jnp.float32).astype(jnp.bfloat16)


def load_block(ref):
    width = ref.shape[0] - META
    parts = [ref[pl.ds(k * LANES, LANES), :] for k in range(width // LANES)]
    meta = ref[pl.ds(width, META), :].astype(jnp.float32)
    return jnp.concatenate(parts, axis=1), meta[0:1], meta[1:2] * 256.0 + meta[2:3]


def down(row):
    return jnp.transpose(jnp.broadcast_to(row, (LANES, LANES)))


def pair_kernel(block, mate, pair):
    step = block.shape[0]
    pair[pl.ds(0, step), :] = block[...]
    pair[pl.ds(step, step), :] = mate[...]


def join(block, mate):
    return pl.pallas_call(
        pair_kernel,
        out_shape=jax.ShapeDtypeStruct((2 * block.shape[0], LANES), block.dtype),
        in_specs=[pl.BlockSpec(memory_space=pltpu.VMEM)] * 2,
        out_specs=pl.BlockSpec(memory_space=pltpu.VMEM),
        compiler_params=pltpu.CompilerParams(vmem_limit_bytes=16 * 2**20),
    )(block, mate)


def score_kernel(queries, places, cross, *refs):
    query_ref, refs = refs[0], refs[1:]
    key_refs, outs = refs[: len(places)], refs[len(places) :]
    step = query_ref.shape[0] // queries
    loaded = [load_block(query_ref.at[pl.ds(i * step, step)]) for i in range(queries)]
    query = jnp.concatenate([block[0] for block in loaded], axis=0)
    q_clu = jnp.concatenate([down(block[1]) for block in loaded], axis=0)
    q_idx = jnp.concatenate([down(block[2]) for block in loaded], axis=0)
    row_best = jnp.full((queries * LANES, LANES), -1.0, jnp.float32)
    for first in range(0, len(places), 2):
        keys = [load_block(ref) for ref in key_refs[first : first + 2]]
        scores = lax.dot_general(
            query,
            jnp.concatenate([key[0] for key in keys], axis=0),
            (((1,), (1,)), ((), ())),
            preferred_element_type=jnp.float32,
        )
        for number, key in enumerate(keys):
            part = scores[:, number * LANES : (number + 1) * LANES]
            part = jnp.where(key[1] == q_clu, part, -1.0)
            earlier = key[2] < q_idx
            row_best = jnp.maximum(row_best, jnp.where(earlier, part, -1.0))
            if cross:
                col = jnp.max(jnp.where(earlier, -1.0, part), axis=0, keepdims=True)
                outs[1][pl.ds(places[first + number], 1), :] = col
    for i in range(queries):
        block = jnp.transpose(row_best[i * LANES : (i + 1) * LANES])
        outs[0][pl.ds(i, 1), :] = jnp.max(block, axis=0, keepdims=True)


def score(count, query, keys, places, cross):
    blocks = len(keys)
    width = keys[0].shape[0] - META
    shapes = [jax.ShapeDtypeStruct((count, LANES), jnp.float32)]
    if cross:
        shapes.append(jax.ShapeDtypeStruct((blocks, LANES), jnp.float32))
    return pl.pallas_call(
        functools.partial(score_kernel, count, places, cross),
        out_shape=shapes,
        in_specs=[pl.BlockSpec(memory_space=pltpu.VMEM)] * (1 + blocks),
        out_specs=[pl.BlockSpec(memory_space=pltpu.VMEM)] * len(shapes),
        compiler_params=pltpu.CompilerParams(vmem_limit_bytes=32 * 2**20),
        cost_estimate=pl.CostEstimate(
            flops=2 * count * blocks * LANES * LANES * width,
            bytes_accessed=2 * (count + blocks) * LANES * width,
            transcendentals=0,
        ),
    )(query, *keys)


def merge_kernel(fold, col, col_other, row_other, own, odd, near, mix, chip):
    def both(p):
        q = (p & ~6 | (p & 2) << 1 | (p & 4) >> 1) ^ 1
        return jnp.maximum(col[pl.ds(p, 1), :], col_other[pl.ds(q, 1), :])

    for i in range(2):
        near[pl.ds(i, 1), :] = both(2 + i)
        if fold:
            row = row_other[pl.ds(1 - i, 1), :]
            mix[pl.ds(i, 1), :] = jnp.where(odd[0] == 1, row, both(6 + i))
        else:
            mix[pl.ds(i, 1), :] = both(6 + i)
    chip[pl.ds(0, 1), :] = jnp.maximum(own[...], both(0))
    chip[pl.ds(1, 1), :] = both(1)


def program(groups, blks, embedding, cluster, doc_index):
    rows, width = embedding.shape

    def swap(x):
        return lax.ppermute(x, "group", [(g, g ^ 1) for g in range(groups)])

    def turn(x, even, odd):
        return lax.ppermute(x, "group", [(g, g ^ (odd if g & 1 else even)) for g in range(groups)])

    order = [i // 2 if i % 2 == 0 else blks - 1 - i // 2 for i in range(blks)]
    rounds = max(1, blks // 4)

    def visit(x, number, back):
        pairs = []
        for g in range(groups):
            shift = number + 1 + (rounds if g & 1 else 0)
            for i in range(blks):
                a, b = order[i], order[(i + shift) % blks]
                a, b = g * blks + a, g * blks + b
                pairs.append((b, a) if back else (a, b))
        return lax.ppermute(x, ("group", "blk"), pairs)

    block = pl.pallas_call(
        pack_kernel,
        out_shape=jax.ShapeDtypeStruct((width + META, LANES), jnp.bfloat16),
        in_specs=[pl.BlockSpec(memory_space=pltpu.HBM)] * 3,
        out_specs=pl.BlockSpec(memory_space=pltpu.VMEM),
        scratch_shapes=[
            pltpu.VMEM((rows, width), embedding.dtype),
            pltpu.VMEM((1, rows), jnp.int32),
            pltpu.VMEM((1, rows), jnp.int32),
            pltpu.SemaphoreType.DMA((3,)),
        ],
        compiler_params=pltpu.CompilerParams(vmem_limit_bytes=16 * 2**20),
    )(embedding, cluster.reshape(1, rows), doc_index.reshape(1, rows))

    mate = swap(block)
    near = turn(block, 2, 4)
    pair = join(block, mate)
    visitors = [visit(pair, number, False) for number in range(rounds)]
    near_mate = turn(mate, 2, 4)
    far = turn(near, 4, 2)
    keys = [block, mate, near, near_mate, swap(near_mate), swap(near), far, swap(far)]
    places = [0, 1, 2, 3, 4, 5, 6, 7]
    bit = 8
    while bit < groups:
        keys = keys + [lax.ppermute(k, "group", [(g, g ^ bit) for g in range(groups)]) for k in keys]
        places = places + [p + bit for p in places]
        bit *= 2

    (own_best,) = score(1, block, keys, places, False)
    rows_back, cols = [], None
    for number, visitor in enumerate(visitors):
        row_best, col_best = score(2, visitor, keys, places, True)
        rows_back.append(row_best)
        cols = col_best if cols is None else jnp.maximum(cols, col_best)

    bit = groups // 2
    while bit > 4:
        cols = jnp.maximum(cols[:bit], turn(cols[bit:], bit, bit))
        bit //= 2

    fold = rounds == 1
    odd = (lax.axis_index("group") & 1).astype(jnp.int32).reshape(1)
    small = jax.ShapeDtypeStruct((2, LANES), jnp.float32)
    near_out, mix_out, chip = pl.pallas_call(
        functools.partial(merge_kernel, fold),
        out_shape=[small] * 3,
        in_specs=[pl.BlockSpec(memory_space=pltpu.VMEM)] * 4
        + [pl.BlockSpec(memory_space=pltpu.SMEM)],
        out_specs=[pl.BlockSpec(memory_space=pltpu.VMEM)] * 3,
        compiler_params=pltpu.CompilerParams(vmem_limit_bytes=4 * 2**20),
    )(cols, swap(cols), swap(rows_back[0]), own_best, odd)
    chip = jnp.maximum(chip, turn(near_out, 2, 4))
    pairs = []
    for g in range(groups):
        for i in range(blks):
            if fold and g & 1:
                pairs.append((g * blks + order[(i + 1) % blks], g * blks + order[i]))
            else:
                pairs.append((g * blks + i, (g ^ 6) * blks + i))
    chip = jnp.maximum(chip, lax.ppermute(mix_out, ("group", "blk"), pairs))
    if not fold:
        for number, row_best in enumerate(rows_back):
            chip = jnp.maximum(chip, visit(row_best, number, True))
    return jnp.maximum(chip[0], swap(chip[1]))


def solution(mesh):
    return jax.shard_map(
        functools.partial(program, mesh.shape["group"], mesh.shape["blk"]),
        mesh=mesh,
        in_specs=(P(("group", "blk"), None), P(("group", "blk")), P(("group", "blk"))),
        out_specs=P(("group", "blk")),
        check_vma=False,
    )
```

```python
import functools

import jax
import jax.numpy as jnp
from jax import lax
from jax.experimental import pallas as pl
from jax.experimental.pallas import tpu as pltpu
from jax.sharding import PartitionSpec as P

LANES = 128
META = 16


def meta_kernel(clu, idx, out):
    row = lax.broadcasted_iota(jnp.int32, (META, LANES), 0)
    index = idx[...]
    meta = jnp.where(row == 0, clu[...], jnp.where(row == 1, index >> 8, index & 255))
    out[...] = meta.astype(jnp.float32).astype(jnp.bfloat16)


def pack_kernel(emb, meta, out):
    width = emb.shape[1]
    wide = emb[...].astype(jnp.float32)
    norm = lax.rsqrt(jnp.sum(wide * wide, axis=1, keepdims=True) + 1e-06)
    unit = (wide * norm).astype(jnp.bfloat16)
    for k in range(width // LANES):
        out[pl.ds(k * LANES, LANES), :] = unit[:, k * LANES : (k + 1) * LANES]
    out[pl.ds(width, META), :] = meta[...]


def load_block(ref):
    width = ref.shape[0] - META
    parts = [ref[pl.ds(k * LANES, LANES), :] for k in range(width // LANES)]
    meta = ref[pl.ds(width, META), :].astype(jnp.float32)
    return jnp.concatenate(parts, axis=1), meta[0:1], meta[1:2] * 256.0 + meta[2:3]


def down(row):
    return jnp.transpose(jnp.broadcast_to(row, (LANES, LANES)))


def pair_kernel(block, mate, pair):
    step = block.shape[0]
    pair[pl.ds(0, step), :] = block[...]
    pair[pl.ds(step, step), :] = mate[...]


def join(block, mate):
    return pl.pallas_call(
        pair_kernel,
        out_shape=jax.ShapeDtypeStruct((2 * block.shape[0], LANES), block.dtype),
        in_specs=[pl.BlockSpec(memory_space=pltpu.VMEM)] * 2,
        out_specs=pl.BlockSpec(memory_space=pltpu.VMEM),
        compiler_params=pltpu.CompilerParams(vmem_limit_bytes=16 * 2**20),
    )(block, mate)


def score_kernel(queries, places, cross, *refs):
    query_ref, refs = refs[0], refs[1:]
    key_refs, out = refs[:-1], refs[-1]
    base = len(places) if cross else 0
    step = query_ref.shape[0] // queries
    loaded = [load_block(query_ref.at[pl.ds(i * step, step)]) for i in range(queries)]
    query = jnp.concatenate([block[0] for block in loaded], axis=0)
    q_clu = jnp.concatenate([down(block[1]) for block in loaded], axis=0)
    q_idx = jnp.concatenate([down(block[2]) for block in loaded], axis=0)
    row_best = jnp.full((queries * LANES, LANES), -1.0, jnp.float32)
    for first in range(0, len(places), 2):
        keys = [load_block(ref) for ref in key_refs[first : first + 2]]
        scores = lax.dot_general(
            query,
            jnp.concatenate([key[0] for key in keys], axis=0),
            (((1,), (1,)), ((), ())),
            preferred_element_type=jnp.float32,
        )
        for number, key in enumerate(keys):
            part = scores[:, number * LANES : (number + 1) * LANES]
            part = jnp.where(key[1] == q_clu, part, -1.0)
            earlier = key[2] < q_idx
            row_best = jnp.maximum(row_best, jnp.where(earlier, part, -1.0))
            if cross:
                col = jnp.max(jnp.where(earlier, -1.0, part), axis=0, keepdims=True)
                out[pl.ds(places[first + number], 1), :] = col
    for i in range(queries):
        block = jnp.transpose(row_best[i * LANES : (i + 1) * LANES])
        out[pl.ds(base + i, 1), :] = jnp.max(block, axis=0, keepdims=True)


def score(count, query, keys, places, cross):
    blocks = len(keys)
    width = keys[0].shape[0] - META
    return pl.pallas_call(
        functools.partial(score_kernel, count, places, cross),
        out_shape=jax.ShapeDtypeStruct((count + blocks * cross, LANES), jnp.float32),
        in_specs=[pl.BlockSpec(memory_space=pltpu.VMEM)] * (1 + blocks),
        out_specs=pl.BlockSpec(memory_space=pltpu.VMEM),
        compiler_params=pltpu.CompilerParams(vmem_limit_bytes=32 * 2**20),
        cost_estimate=pl.CostEstimate(
            flops=2 * count * blocks * LANES * LANES * width,
            bytes_accessed=2 * (count + blocks) * LANES * width,
            transcendentals=0,
        ),
    )(query, *keys)


def merge_kernel(fold, res, other, own, near, mix, chip):
    def both(p):
        q = (p & ~6 | (p & 2) << 1 | (p & 4) >> 1) ^ 1
        return jnp.maximum(res[pl.ds(p, 1), :], other[pl.ds(q, 1), :])

    for i in range(2):
        near[pl.ds(i, 1), :] = both(2 + i)
        mix[pl.ds(i, 1), :] = both(6 + i)
    if fold:
        odd = lax.axis_index("group") & 1

        @pl.when(odd == 1)
        def _():
            for i in range(2):
                mix[pl.ds(i, 1), :] = other[pl.ds(9 - i, 1), :]

    chip[pl.ds(0, 1), :] = jnp.maximum(own[...], both(0))
    chip[pl.ds(1, 1), :] = both(1)


def program(groups, blks, embedding, cluster, doc_index):
    rows, width = embedding.shape

    def swap(x):
        return lax.ppermute(x, "group", [(g, g ^ 1) for g in range(groups)])

    def turn(x, even, odd):
        return lax.ppermute(x, "group", [(g, g ^ (odd if g & 1 else even)) for g in range(groups)])

    order = [i // 2 if i % 2 == 0 else blks - 1 - i // 2 for i in range(blks)]
    rounds = max(1, blks // 4)

    def visit(x, number, back):
        pairs = []
        for g in range(groups):
            shift = number + 1 + (rounds if g & 1 else 0)
            for i in range(blks):
                a, b = order[i], order[(i + shift) % blks]
                a, b = g * blks + a, g * blks + b
                pairs.append((b, a) if back else (a, b))
        return lax.ppermute(x, ("group", "blk"), pairs)

    meta = pl.pallas_call(
        meta_kernel,
        out_shape=jax.ShapeDtypeStruct((META, LANES), jnp.bfloat16),
        in_specs=[pl.BlockSpec(memory_space=pltpu.VMEM)] * 2,
        out_specs=pl.BlockSpec(memory_space=pltpu.VMEM),
        compiler_params=pltpu.CompilerParams(vmem_limit_bytes=4 * 2**20),
    )(cluster.reshape(1, rows), doc_index.reshape(1, rows))
    block = pl.pallas_call(
        pack_kernel,
        out_shape=jax.ShapeDtypeStruct((width + META, LANES), jnp.bfloat16),
        in_specs=[pl.BlockSpec(memory_space=pltpu.VMEM)] * 2,
        out_specs=pl.BlockSpec(memory_space=pltpu.VMEM),
        compiler_params=pltpu.CompilerParams(vmem_limit_bytes=16 * 2**20),
    )(embedding, meta)

    mate = swap(block)
    near = turn(block, 2, 4)
    pair = join(block, mate)
    visitors = [visit(pair, number, False) for number in range(rounds)]
    near_mate = turn(mate, 2, 4)
    far = turn(near, 4, 2)
    keys = [block, mate, near, near_mate, swap(near_mate), swap(near), far, swap(far)]
    places = [0, 1, 2, 3, 4, 5, 6, 7]
    bit = 8
    while bit < groups:
        keys = keys + [lax.ppermute(k, "group", [(g, g ^ bit) for g in range(groups)]) for k in keys]
        places = places + [p + bit for p in places]
        bit *= 2

    own_best = score(1, block, keys, places, False)
    results = [score(2, visitor, keys, places, True) for visitor in visitors]
    res = results[0]
    for result in results[1:]:
        res = jnp.maximum(res, result)

    bit = groups // 2
    while bit > 4:
        far_cols = turn(res[bit : 2 * bit], bit, bit)
        res = jnp.concatenate([jnp.maximum(res[:bit], far_cols), res[2 * bit :]])
        bit //= 2

    fold = rounds == 1
    small = jax.ShapeDtypeStruct((2, LANES), jnp.float32)
    near_out, mix_out, chip = pl.pallas_call(
        functools.partial(merge_kernel, fold),
        out_shape=[small] * 3,
        in_specs=[pl.BlockSpec(memory_space=pltpu.VMEM)] * 3,
        out_specs=[pl.BlockSpec(memory_space=pltpu.VMEM)] * 3,
        compiler_params=pltpu.CompilerParams(vmem_limit_bytes=4 * 2**20),
    )(res, swap(res), own_best)
    chip = jnp.maximum(chip, turn(near_out, 2, 4))
    pairs = []
    for g in range(groups):
        for i in range(blks):
            if fold and g & 1:
                pairs.append((g * blks + order[(i + 1) % blks], g * blks + order[i]))
            else:
                pairs.append((g * blks + i, (g ^ 6) * blks + i))
    chip = jnp.maximum(chip, lax.ppermute(mix_out, ("group", "blk"), pairs))
    if not fold:
        for number, result in enumerate(results):
            chip = jnp.maximum(chip, visit(result[groups : groups + 2], number, True))
    return jnp.maximum(chip[0], swap(chip[1]))


def solution(mesh):
    return jax.shard_map(
        functools.partial(program, mesh.shape["group"], mesh.shape["blk"]),
        mesh=mesh,
        in_specs=(P(("group", "blk"), None), P(("group", "blk")), P(("group", "blk"))),
        out_specs=P(("group", "blk")),
        check_vma=False,
    )
```

```python
import functools

import jax
import jax.numpy as jnp
from jax import lax
from jax.experimental import pallas as pl
from jax.experimental.pallas import tpu as pltpu
from jax.sharding import PartitionSpec as P

LANES = 128
META = 16


def meta_kernel(clu, idx, out):
    row = lax.broadcasted_iota(jnp.int32, (META, LANES), 0)
    index = idx[...]
    meta = jnp.where(row == 0, clu[...], jnp.where(row == 1, index >> 8, index & 255))
    out[...] = meta.astype(jnp.float32).astype(jnp.bfloat16)


def pack_kernel(emb, meta, out):
    width = emb.shape[1]
    wide = emb[...].astype(jnp.float32)
    norm = lax.rsqrt(jnp.sum(wide * wide, axis=1, keepdims=True) + 1e-06)
    unit = (wide * norm).astype(jnp.bfloat16)
    for k in range(width // LANES):
        out[pl.ds(k * LANES, LANES), :] = unit[:, k * LANES : (k + 1) * LANES]
    out[pl.ds(width, META), :] = meta[...]


def load_block(ref):
    width = ref.shape[0] - META
    parts = [ref[pl.ds(k * LANES, LANES), :] for k in range(width // LANES)]
    meta = ref[pl.ds(width, META), :].astype(jnp.float32)
    return jnp.concatenate(parts, axis=1), meta[0:1], meta[1:2] * 256.0 + meta[2:3]


def down(row):
    return jnp.transpose(jnp.broadcast_to(row, (LANES, LANES)))


def pair_kernel(block, mate, pair):
    step = block.shape[0]
    pair[pl.ds(0, step), :] = block[...]
    pair[pl.ds(step, step), :] = mate[...]


def join(block, mate):
    return pl.pallas_call(
        pair_kernel,
        out_shape=jax.ShapeDtypeStruct((2 * block.shape[0], LANES), block.dtype),
        in_specs=[pl.BlockSpec(memory_space=pltpu.VMEM)] * 2,
        out_specs=pl.BlockSpec(memory_space=pltpu.VMEM),
        compiler_params=pltpu.CompilerParams(vmem_limit_bytes=16 * 2**20),
    )(block, mate)


def score_kernel(queries, places, cross, *refs):
    query_ref, refs = refs[0], refs[1:]
    key_refs, out = refs[:-1], refs[-1]
    base = len(places) if cross else 0
    step = query_ref.shape[0] // queries
    loaded = [load_block(query_ref.at[pl.ds(i * step, step)]) for i in range(queries)]
    query = jnp.concatenate([block[0] for block in loaded], axis=0)
    q_clu = jnp.concatenate([down(block[1]) for block in loaded], axis=0)
    q_idx = jnp.concatenate([down(block[2]) for block in loaded], axis=0)
    row_best = jnp.full((queries * LANES, LANES), -1.0, jnp.float32)
    for first in range(0, len(places), 2):
        keys = [load_block(ref) for ref in key_refs[first : first + 2]]
        scores = lax.dot_general(
            query,
            jnp.concatenate([key[0] for key in keys], axis=0),
            (((1,), (1,)), ((), ())),
            preferred_element_type=jnp.float32,
        )
        for number, key in enumerate(keys):
            part = scores[:, number * LANES : (number + 1) * LANES]
            part = jnp.where(key[1] == q_clu, part, -1.0)
            earlier = key[2] < q_idx
            row_best = jnp.maximum(row_best, jnp.where(earlier, part, -1.0))
            if cross:
                col = jnp.max(jnp.where(earlier, -1.0, part), axis=0, keepdims=True)
                out[pl.ds(places[first + number], 1), :] = col
    for i in range(queries):
        block = jnp.transpose(row_best[i * LANES : (i + 1) * LANES])
        out[pl.ds(base + i, 1), :] = jnp.max(block, axis=0, keepdims=True)


def score(count, query, keys, places, cross):
    blocks = len(keys)
    width = keys[0].shape[0] - META
    return pl.pallas_call(
        functools.partial(score_kernel, count, places, cross),
        out_shape=jax.ShapeDtypeStruct((count + blocks * cross, LANES), jnp.float32),
        in_specs=[pl.BlockSpec(memory_space=pltpu.VMEM)] * (1 + blocks),
        out_specs=pl.BlockSpec(memory_space=pltpu.VMEM),
        compiler_params=pltpu.CompilerParams(vmem_limit_bytes=32 * 2**20),
        cost_estimate=pl.CostEstimate(
            flops=2 * count * blocks * LANES * LANES * width,
            bytes_accessed=2 * (count + blocks) * LANES * width,
            transcendentals=0,
        ),
    )(query, *keys)


def merge_kernel(fold, res, other, near, side, mix, home):
    def both(p):
        q = (p & ~6 | (p & 2) << 1 | (p & 4) >> 1) ^ 1
        return jnp.maximum(res[pl.ds(p, 1), :], other[pl.ds(q, 1), :])

    near[...] = both(2)
    side[...] = both(4)
    for i in range(2):
        mix[pl.ds(i, 1), :] = both(6 + i)
    if fold:
        odd = lax.axis_index("group") & 1

        @pl.when(odd == 1)
        def _():
            for i in range(2):
                mix[pl.ds(i, 1), :] = other[pl.ds(9 - i, 1), :]

    home[...] = both(0)


def program(groups, blks, embedding, cluster, doc_index):
    rows, width = embedding.shape

    def swap(x):
        return lax.ppermute(x, "group", [(g, g ^ 1) for g in range(groups)])

    def turn(x, even, odd):
        return lax.ppermute(x, "group", [(g, g ^ (odd if g & 1 else even)) for g in range(groups)])

    order = [i // 2 if i % 2 == 0 else blks - 1 - i // 2 for i in range(blks)]
    rounds = max(1, blks // 4)

    def visit(x, number, back):
        pairs = []
        for g in range(groups):
            shift = number + 1 + (rounds if g & 1 else 0)
            for i in range(blks):
                a, b = order[i], order[(i + shift) % blks]
                a, b = g * blks + a, g * blks + b
                pairs.append((b, a) if back else (a, b))
        return lax.ppermute(x, ("group", "blk"), pairs)

    meta = pl.pallas_call(
        meta_kernel,
        out_shape=jax.ShapeDtypeStruct((META, LANES), jnp.bfloat16),
        in_specs=[pl.BlockSpec(memory_space=pltpu.VMEM)] * 2,
        out_specs=pl.BlockSpec(memory_space=pltpu.VMEM),
        compiler_params=pltpu.CompilerParams(vmem_limit_bytes=4 * 2**20),
    )(cluster.reshape(1, rows), doc_index.reshape(1, rows))
    block = pl.pallas_call(
        pack_kernel,
        out_shape=jax.ShapeDtypeStruct((width + META, LANES), jnp.bfloat16),
        in_specs=[pl.BlockSpec(memory_space=pltpu.VMEM)] * 2,
        out_specs=pl.BlockSpec(memory_space=pltpu.VMEM),
        compiler_params=pltpu.CompilerParams(vmem_limit_bytes=16 * 2**20),
    )(embedding, meta)

    mate = swap(block)
    near = turn(block, 2, 4)
    pair = join(block, mate)
    visitors = [visit(pair, number, False) for number in range(rounds)]
    near_mate = turn(mate, 2, 4)
    far = turn(near, 4, 2)
    keys = [block, mate, near, near_mate, swap(near_mate), swap(near), far, swap(far)]
    places = [0, 1, 2, 3, 4, 5, 6, 7]
    bit = 8
    while bit < groups:
        keys = keys + [lax.ppermute(k, "group", [(g, g ^ bit) for g in range(groups)]) for k in keys]
        places = places + [p + bit for p in places]
        bit *= 2

    own_best = score(1, block, keys, places, False)
    results = [score(2, visitor, keys, places, True) for visitor in visitors]
    res = results[0]
    for result in results[1:]:
        res = jnp.maximum(res, result)

    bit = groups // 2
    while bit > 4:
        far_cols = turn(res[bit : 2 * bit], bit, bit)
        res = jnp.concatenate([jnp.maximum(res[:bit], far_cols), res[2 * bit :]])
        bit //= 2

    fold = rounds == 1
    one = jax.ShapeDtypeStruct((1, LANES), jnp.float32)
    two = jax.ShapeDtypeStruct((2, LANES), jnp.float32)
    near_out, side_out, mix_out, home = pl.pallas_call(
        functools.partial(merge_kernel, fold),
        out_shape=[one, one, two, one],
        in_specs=[pl.BlockSpec(memory_space=pltpu.VMEM)] * 2,
        out_specs=[pl.BlockSpec(memory_space=pltpu.VMEM)] * 4,
        compiler_params=pltpu.CompilerParams(vmem_limit_bytes=4 * 2**20),
    )(res, swap(res))
    pairs = []
    for g in range(groups):
        for i in range(blks):
            if fold and g & 1:
                pairs.append((g * blks + order[(i + 1) % blks], g * blks + order[i]))
            else:
                pairs.append((g * blks + i, (g ^ 6) * blks + i))
    mixed = lax.ppermute(mix_out, ("group", "blk"), pairs)
    best = jnp.maximum(jnp.maximum(home[0], own_best[0]), turn(near_out[0], 2, 4))
    best = jnp.maximum(best, turn(side_out[0], 4, 2))
    if not fold:
        for number, result in enumerate(results):
            mixed = jnp.maximum(mixed, visit(result[groups : groups + 2], number, True))
    return jnp.maximum(jnp.maximum(best, mixed[0]), swap(mixed[1]))


def solution(mesh):
    return jax.shard_map(
        functools.partial(program, mesh.shape["group"], mesh.shape["blk"]),
        mesh=mesh,
        in_specs=(P(("group", "blk"), None), P(("group", "blk")), P(("group", "blk"))),
        out_specs=P(("group", "blk")),
        check_vma=False,
    )
```
